256 devices in a mesh: seq: 32 (over x_hi, z, core), head: 8 (over x_lo, y).
Axes of the slice: x: 4 (x_hi: 2, x_lo: 2; x = x_hi * 2 + x_lo), y: 4, z: 8, core: 2. Of those that a mesh axis runs over, the one named last changes fastest.
Arguments:
- queries: bfloat16 [64, 32, 4096], P('seq', None, 'head'), may hold values from -39 to 39
- new_kv: bfloat16 [64, 32, 2, 1024], P('seq', None, None, 'head'), may hold values from -6 to 6
- cache: bfloat16 [32, 4096, 2, 1024], P('seq', None, None, 'head'), may hold values from -6 to 6
- sinks: bfloat16 [32, 4, 2, 1024], P(None, None, None, 'head'), may hold values from -16 to 16
- lengths: int32 [32], replicated, may hold values from 6 to 32768, as said below
- offsets: int32 [32], replicated, may hold values from 0 to 4095
- order: int32 [32], replicated, may hold values from 0 to 31, as said below
- residual: bfloat16 [64, 32, 4096], P('seq', None, 'head'), may hold values from -16 to 16
- o_weight: bfloat16 [4096, 4096], P('head', 'seq'), may hold values from -0.1875 to 0.1875
- ffn_gain: float32 [4096], P('head'), may hold values from 0.1 to 1.9
- router: float32 [4096, 8], P('head'), may hold values from -0.09375 to 0.09375
- expert_ids: int32 [64, 32, 2], P('seq'), may hold values from 0 to 7, all different within a row; in each aligned block of 64 rows (0 to 63, 64 to 127, ..., all dimensions but the last counted through in order) at most 18 rows name the same one
- w_in: bfloat16 [8, 4096, 2, 8192], P('head', None, None, 'seq'), may hold values from -0.09375 to 0.09375
- w_out: bfloat16 [8, 8192, 4096], P('head', 'seq'), may hold values from -0.0625 to 0.0625
Outputs:
- layer_out: bfloat16 [64, 32, 4096], P('seq', None, 'head')
- cache_out: bfloat16 [32, 4096, 2, 1024], P('seq', None, None, 'head')
The draws below stay inside these ranges and needn't reach their ends.
Inputs may be any that keep to these rules, and one draw needn't show every extreme that they name: `lengths`: one request has exactly 32768 cached tokens and one exactly 6; the others are spread below 1024, 4096 and 32768. `order`: a permutation. `expert_ids`: each row names two different experts; among the 64 rows of one index of seq (an aligned block of the flattened token grid of 64 x 32) no expert is named more than 18 times.
All inputs are finite; a program needn't handle non-finite values.
Results may differ from the reference program's by a relative error of at most 0.015.
Values may be sent and summed in bfloat16 or wider, within the bound.
No kernel may reach another device: no remote copies, remote signals or barrier semaphores. Data moves between devices by JAX's collectives and lax.ppermute only.
A program may use at most 64 MiB of HBM per device.

```python
import math
from functools import partial
import jax
import jax.numpy as jnp
import numpy as np
from jax import lax

D = 4096
H = 32
KVH = 8
HD = 128
FF = 8192
E = 8
SINK = 4
W = 4096
MAXLEN = 32768
C = 64
R = 32
CAP = 18
N_SEQ = 32


def cycle_lengths(key):
    base_key = jax.random.fold_in(key, 101)
    class_key, value_key, pick_key = jax.random.split(base_key, 3)
    classes = jax.random.randint(class_key, (R,), 0, 3)
    ceiling = jnp.where(classes == 0, W // 4, jnp.where(classes == 1, W, MAXLEN))
    raw_values = jax.random.randint(value_key, (R,), 0, 1 << 30)
    result = raw_values % (ceiling - SINK - 1) + SINK + 2
    chosen = jax.random.permutation(pick_key, R)
    result = result.at[chosen[0]].set(MAXLEN).at[chosen[1]].set(SINK + 2)
    return result.astype(jnp.int32)


def cycle_offsets(key):
    base_key = jax.random.fold_in(key, 202)
    value_key, pick_key = jax.random.split(base_key, 2)
    result = jax.random.randint(value_key, (R,), 0, W)
    chosen = jax.random.permutation(pick_key, R)
    result = result.at[chosen[0]].set(W - 1).at[chosen[1]].set(0)
    return result.astype(jnp.int32)


def batch_order(key):
    return jax.random.permutation(jax.random.fold_in(key, 404), R).astype(jnp.int32)


def draw_lengths(key, part):
    return cycle_lengths(key)


def draw_offsets(key, part):
    return cycle_offsets(key)


def draw_order(key, part):
    return batch_order(key)


def draw_cache(key, part):
    shape = (R, W, 2, KVH * HD)
    value_key = jax.random.fold_in(key, 303)
    values = jnp.clip(jax.random.normal(value_key, shape, jnp.float32), -6.0, 6.0)
    return values.astype(jnp.bfloat16)


def draw_queries(key, part):
    shape = (C, R, H * HD)
    value_key = jax.random.fold_in(key, 505)
    values = jnp.clip(jax.random.normal(value_key, shape, jnp.float32), -6.0, 6.0)
    return values.astype(jnp.bfloat16)


def draw_residual(key, part):
    shape = (C, R, D)
    value_key = jax.random.fold_in(key, 808)
    column = jnp.arange(D, dtype=jnp.float32) / max(D - 1, 1)
    values = jnp.clip(jax.random.normal(value_key, shape, jnp.float32), -6.0, 6.0) * 0.1 * 3.0 ** column
    return values.astype(jnp.bfloat16)


def raised(array, key, source, target, shards_of, factor):
    owner, partner = [(jnp.arange(array.shape[axis_at]) // (array.shape[axis_at] // shards_of)).reshape([-1 if axis == axis_at else 1 for axis in range(array.ndim)]) for axis_at in (source, target)]
    chosen = jax.random.permutation(key, shards_of)[partner]
    strong = (owner == chosen) | (owner == (partner + shards_of // 2) % shards_of)
    return jnp.where(strong, factor * array, array)


def shard_levels(rng, dims, cuts, smallest, largest):
    level, own = 1.0, jax.random.fold_in(rng, 6)
    for dim, parts in cuts:
        draws = jnp.exp(jax.random.uniform(jax.random.fold_in(own, dim), (parts,), jnp.float32, smallest / len(cuts), largest / len(cuts)))
        level = level * jnp.repeat(draws, dims[dim] // parts).reshape([-1 if axis == dim else 1 for axis in range(len(dims))])
    return level


def assign_block(key, own, number, rows, count, top, most, slope):
    order = jax.random.permutation(key, count)
    crowded, usual = load_shares(count, rows * top, most, slope, True), load_shares(count, rows * top, most, slope, False)
    places = jnp.arange(count)

    def named(sizes, offset_by):
        used = int((sizes > 0).sum())
        fixed = max(1, used // 4)
        shifted = fixed + (places - fixed + offset_by * (used - fixed)) % max(1, count - fixed)
        return jnp.zeros((count,), jnp.int32).at[order[jnp.where(places < fixed, places, shifted)]].set(jnp.asarray(sizes, jnp.int32))

    sizes = jnp.where(number % 4 == 0, named(crowded, number // 4), named(usual, number - number // 4 - 1))
    mixed = jax.random.permutation(jax.random.fold_in(own, 3), count)
    donor, sink = mixed[0:count // 2 * 2:2], mixed[1:count // 2 * 2:2]
    margin = jnp.minimum(sizes[donor] - 1, most - sizes[sink]) // 2
    margin = jnp.where((donor == order[0]) | (sink == order[0]) | (sizes[sink] == 0), 0, jnp.maximum(margin, 0))
    shifted = jax.random.randint(jax.random.fold_in(own, 4), (count // 2,), 0, 1 << 20) % (margin + 1)
    sizes = sizes.at[donor].add(-shifted).at[sink].add(shifted)
    labels = jnp.searchsorted(jnp.cumsum(sizes), jnp.arange(rows * top), side="right").astype(jnp.int32)
    table = labels.reshape(top, rows).T
    table = table[jax.random.permutation(jax.random.fold_in(own, 1), rows)]
    offset_by = jax.random.randint(jax.random.fold_in(own, 2), (rows, 1), 0, top)
    return jnp.take_along_axis(table, (jnp.arange(top)[None, :] + offset_by) % top, axis=1)


def load_shares(count, total, bound, lean, full):
    weights = [(1 << 20) // math.isqrt(standing ** lean) + 1 for standing in range(1, count + 1)]
    largest = bound if full else min(bound, max(-(-total // count), total * weights[0] // sum(weights)))
    least = 1 if total - largest >= count - 1 else 0
    counts, rest = [largest] + [least] * (count - 1), total - largest - least * (count - 1)
    while rest > 0:
        candidates = [i for i in range(1, count) if counts[i] < largest] or [i for i in range(1, count) if counts[i] < bound]
        pool, budget = sum([weights[i] for i in candidates]), rest
        for i in candidates:
            more = min(bound - counts[i], max(1, budget * weights[i] // pool), rest)
            counts[i] = counts[i] + more
            rest = rest - more
    return np.array(counts)


def noise(own_key, extent, spread, bound, cuts=(), held_as=jnp.bfloat16):
    loudness = shard_levels(own_key, extent, cuts, -0.22, 0.18) if cuts else 1.0
    array = jax.random.normal(own_key, extent, jnp.float32) * spread * loudness
    return jnp.minimum(jnp.maximum(array, -bound), bound).astype(held_as)


def bell_draw_with(stream_key, extent, width, reach, cuts, heavy, kind=jnp.bfloat16):
    values = width * jax.random.normal(stream_key, extent, jnp.float32)
    if cuts:
        values = values * shard_levels(stream_key, extent, cuts, -0.22, 0.18)
    return jnp.clip(raised(values, jax.random.fold_in(stream_key, 3), *heavy), -reach, reach).astype(kind)


def setup_inputs(seed: int = 0) -> dict:
    streams_of = jax.random.split(jax.random.key(seed), 15)
    queries = draw_queries(jax.random.fold_in(streams_of[14], 71), 0)
    new_kv = noise(streams_of[1], (C, R, 2, KVH * HD), 1.0, 6.0, ((0, 32), (3, 8)))
    cache = draw_cache(jax.random.fold_in(streams_of[14], 71), 0)
    sinks = noise(streams_of[3], (R, SINK, 2, KVH * HD), 3.5, 16.0, ((3, 8),))
    lengths = draw_lengths(jax.random.fold_in(streams_of[14], 71), 0)
    offsets = draw_offsets(jax.random.fold_in(streams_of[14], 71), 0)
    order = draw_order(jax.random.fold_in(streams_of[14], 71), 0)
    residual = draw_residual(jax.random.fold_in(streams_of[14], 71), 0)
    o_weight = bell_draw_with(streams_of[8], (H * HD, D), (H * HD) ** -0.5, 0.1875, ((0, 8), (1, 32)), (0, 1, 32, 2.75))
    ffn_gain = jnp.clip(1.0 + 0.18 * jax.random.normal(streams_of[9], (D,), jnp.float32), 0.1, 1.9)
    router = noise(streams_of[10], (D, E), D ** -0.5, 0.09375, ((0, 8),), jnp.float32)
    expert_ids_keys = jax.random.split(jax.random.fold_in(streams_of[11], 1), C * R // C)
    expert_ids_turns = jax.random.permutation(jax.random.fold_in(streams_of[11], 3), C * R // C)
    expert_ids = jax.vmap(lambda own, number: assign_block(jax.random.fold_in(streams_of[11], 2), own, number, C, E, 2, CAP, 1))(expert_ids_keys, expert_ids_turns).reshape((C, R, 2))
    w_in = noise(streams_of[12], (E, D, 2, FF), D ** -0.5, 0.09375, ((0, 8), (3, 32)))
    w_out = noise(streams_of[13], (E, FF, D), FF ** -0.5, 0.0625, ((0, 8), (1, 32)))
    return {"queries": queries, "new_kv": new_kv, "cache": cache, "sinks": sinks, "lengths": lengths, "offsets": offsets, "order": order, "residual": residual, "o_weight": o_weight, "ffn_gain": ffn_gain, "router": router, "expert_ids": expert_ids, "w_in": w_in, "w_out": w_out}


def attend_slot(slot_index, queries, new_kv, cache, sinks, lengths, offsets, order):
    request = order[slot_index]
    length = lengths[request]
    offset = offsets[request]
    group_size = H // KVH
    query_rows = queries[:, slot_index].astype(jnp.float32).reshape(C, KVH, group_size, HD)
    cycle_rows = cache[request]
    sink_rows = sinks[request]
    span_rows = new_kv[:, slot_index]
    key_rows = jnp.concatenate([sink_rows[:, 0], cycle_rows[:, 0], span_rows[:, 0]], 0)
    key_rows = key_rows.astype(jnp.float32).reshape(-1, KVH, HD)
    value_rows = jnp.concatenate([sink_rows[:, 1], cycle_rows[:, 1], span_rows[:, 1]], 0)
    value_rows = value_rows.astype(jnp.float32).reshape(-1, KVH, HD)
    token_pos = jnp.arange(C, dtype=jnp.int32)
    cycle_age = (jnp.arange(W, dtype=jnp.int32) - offset) % W
    cycle_live = (cycle_age[None, :] > token_pos[:, None]) & (cycle_age[None, :] >= W - length + SINK)
    span_live = token_pos[None, :] <= token_pos[:, None]
    visible = jnp.concatenate([jnp.ones((C, SINK), dtype=bool), cycle_live, span_live], 1)
    scores = jnp.einsum('cgjd,kgd->gjck', query_rows, key_rows) * HD ** (-0.5)
    scores = jnp.where(visible[None, None], scores, -jnp.inf)
    row_max = lax.optimization_barrier(jnp.max(scores, -1, keepdims=True))
    expo = jnp.exp(scores - row_max)
    total = lax.optimization_barrier(jnp.sum(expo, -1, keepdims=True))
    weights = lax.optimization_barrier(expo.astype(jnp.bfloat16)).astype(jnp.float32)
    mixed = jnp.einsum('gjck,kgd->gjcd', weights, value_rows) / total
    return mixed.transpose(2, 0, 1, 3).reshape(C, H * HD).astype(jnp.bfloat16)

def run_expert(expert, buckets, w_in, w_out):
    block_width = FF // N_SEQ
    rows_in = buckets[:, expert]
    gate_up = jnp.dot(rows_in, w_in[expert].reshape(D, 2 * FF), preferred_element_type=jnp.float32)
    inner = (jax.nn.silu(gate_up[:, :FF]) * gate_up[:, FF:]).astype(jnp.bfloat16)
    down = w_out[expert]

    def add_block(accum, block_index):
        start_col = (block_index * block_width).astype(jnp.int32)
        inner_block = lax.dynamic_slice_in_dim(inner, start_col, block_width, 1)
        down_block = lax.dynamic_slice_in_dim(down, start_col, block_width, 0)
        term = jnp.dot(inner_block, down_block, preferred_element_type=jnp.float32)
        term = lax.optimization_barrier(term.astype(jnp.bfloat16)).astype(jnp.float32)
        return (accum + term, None)
    accum, _ = lax.scan(add_block, jnp.zeros((rows_in.shape[0], D), jnp.float32), jnp.arange(N_SEQ, dtype=jnp.int32))
    return accum.astype(jnp.bfloat16)

def reference(queries, new_kv, cache, sinks, lengths, offsets, order, residual, o_weight, ffn_gain, router, expert_ids, w_in, w_out):
    attend = partial(attend_slot, queries=queries, new_kv=new_kv, cache=cache, sinks=sinks, lengths=lengths, offsets=offsets, order=order)
    attended = lax.map(attend, jnp.arange(R, dtype=jnp.int32))
    attended = jnp.transpose(attended, (1, 0, 2)).reshape(C * R, H * HD)
    projected = jnp.dot(attended, o_weight, preferred_element_type=jnp.float32)
    hidden_sum = residual.reshape(C * R, D).astype(jnp.float32) + projected
    inv_rms = lax.rsqrt(lax.optimization_barrier(jnp.mean(hidden_sum * hidden_sum, -1)) + 1e-05)
    gained = hidden_sum * ffn_gain
    normed = (gained * inv_rms[:, None]).astype(jnp.bfloat16)
    logits = inv_rms[:, None] * jnp.dot(gained, router, precision=lax.Precision.HIGHEST)
    picks = expert_ids.reshape(C * R, 2).astype(jnp.int32)
    expert_iota = jnp.arange(E, dtype=jnp.int32)
    first_hot = picks[:, 0:1] == expert_iota[None, :]
    second_hot = picks[:, 1:2] == expert_iota[None, :]
    first_logit = lax.optimization_barrier(jnp.sum(jnp.where(first_hot, logits, 0.0), -1))
    second_logit = lax.optimization_barrier(jnp.sum(jnp.where(second_hot, logits, 0.0), -1))
    gate_one = jax.nn.sigmoid(first_logit - second_logit).astype(jnp.bfloat16)
    gate_two = jax.nn.sigmoid(second_logit - first_logit).astype(jnp.bfloat16)
    both_hot = (first_hot | second_hot).astype(jnp.int32).reshape(N_SEQ, C, E)
    earlier = (jnp.cumsum(both_hot, 1) - both_hot).reshape(C * R, E)
    slot_one = lax.optimization_barrier(jnp.sum(jnp.where(first_hot, earlier, 0), -1)).astype(jnp.int32)
    slot_two = lax.optimization_barrier(jnp.sum(jnp.where(second_hot, earlier, 0), -1)).astype(jnp.int32)
    block_of = jnp.arange(C * R, dtype=jnp.int32) // C
    row_one = block_of * CAP + slot_one
    row_two = block_of * CAP + slot_two
    buckets = jnp.zeros((N_SEQ * CAP * E, D), jnp.bfloat16)
    buckets = buckets.at[row_one * E + picks[:, 0]].set(normed).at[row_two * E + picks[:, 1]].set(normed)
    buckets = buckets.reshape(N_SEQ * CAP, E, D)
    experts_out = lax.map(partial(run_expert, buckets=buckets, w_in=w_in, w_out=w_out), jnp.arange(E, dtype=jnp.int32))
    out_one = experts_out[picks[:, 0], row_one].astype(jnp.float32)
    out_two = experts_out[picks[:, 1], row_two].astype(jnp.float32)
    layer = hidden_sum + gate_one.astype(jnp.float32)[:, None] * out_one + gate_two.astype(jnp.float32)[:, None] * out_two
    layer = layer.astype(jnp.bfloat16).reshape(C, R, D)
    inverse = jnp.zeros((R,), jnp.int32).at[order].set(jnp.arange(R, dtype=jnp.int32))
    layer_out = jnp.take(layer, inverse, axis=1)
    new_request = jnp.transpose(jnp.take(new_kv, inverse, axis=1), (1, 0, 2, 3))
    token_of = (jnp.arange(W, dtype=jnp.int32)[None, :] - offsets[:, None]) % W
    picked = jnp.take_along_axis(new_request, jnp.minimum(token_of, C - 1)[:, :, None, None], axis=1)
    cache_out = jnp.where((token_of < C)[:, :, None, None], picked, cache)
    return (layer_out, cache_out)
```

```python
import functools

import jax
import jax.numpy as jnp
from jax import lax
from jax.experimental import pallas as pl
from jax.experimental.pallas import tpu as pltpu
from jax.sharding import Mesh
from jax.sharding import PartitionSpec as P

D = 4096
HD = 128
E = 8
CAP = 18
SLOT = 24
NZ = 8
BF = jnp.bfloat16
F32 = jnp.float32
VMEM = pl.BlockSpec(memory_space=pltpu.VMEM)
SMEM = pl.BlockSpec(memory_space=pltpu.SMEM)
SEQ = ("xh", "z", "c")
HEAD = ("xl", "y")


def call(body, outs, name, n_in, scalars=0, flops=0, nbytes=0, limit=32, scratch=()):
    return pl.pallas_call(
        body,
        out_shape=outs,
        in_specs=[SMEM] * scalars + [VMEM] * (n_in - scalars),
        out_specs=jax.tree.map(lambda _: VMEM, outs),
        scratch_shapes=list(scratch),
        compiler_params=pltpu.CompilerParams(vmem_limit_bytes=limit << 20),
        cost_estimate=pl.CostEstimate(
            flops=flops, bytes_accessed=nbytes, transcendentals=0
        ),
        name=name,
    )


def shape(*dims, dtype=BF):
    return jax.ShapeDtypeStruct(dims, dtype)


def dot(a, b):
    return jnp.dot(a, b, preferred_element_type=F32)


def dot_t(a, b):
    return lax.dot_general(a, b, (((1,), (1,)), ((), ())), preferred_element_type=F32)


def slot_of_request(order_row):
    n = order_row.shape[1]
    return order_row == lax.broadcasted_iota(jnp.int32, (n, n), 0)


def permute_body(order_ref, q_ref, kv_ref, out_ref):
    hot = jnp.where(slot_of_request(order_ref[...]), 1.0, 0.0).astype(BF)
    for i in range(q_ref.shape[0]):
        out_ref[i, :, 0:512] = dot(hot, q_ref[i]).astype(BF)
        out_ref[i, :, 512:768] = dot(hot, kv_ref[i]).astype(BF)


def split_body(cache_ref, k_ref, v_ref, wide):
    rows = cache_ref.shape[0]
    wide[...] = cache_ref[...].astype(F32)
    k_ref[...] = wide[pl.ds(0, rows // 2, stride=2), :].astype(BF)
    v_ref[...] = wide[pl.ds(1, rows // 2, stride=2), :].astype(BF)


def split_cycle(cache_rows):
    rows, step = cache_rows.shape[0], 2048
    return pl.pallas_call(
        split_body,
        grid=(rows // step,),
        out_shape=[shape(rows // 2, HD)] * 2,
        in_specs=[pl.BlockSpec((step, HD), lambda n: (n, 0))],
        out_specs=[pl.BlockSpec((step // 2, HD), lambda n: (n, 0))] * 2,
        scratch_shapes=[pltpu.VMEM((step, HD), F32)],
        cost_estimate=pl.CostEstimate(
            flops=1 << 24, bytes_accessed=8 << 20, transcendentals=0
        ),
        name="split_cycle",
    )(cache_rows)


CHUNK = 512


def attend_body(
    seq_ref, len_ref, off_ref, rows_ref, k_ref, v_ref, sink_ref, out_ref, scores, wide
):
    seq = seq_ref[0]
    length, offset = len_ref[seq], off_ref[seq]
    span = rows_ref.shape[0]
    cycle = k_ref.shape[0]
    group = 4
    query = jnp.concatenate(
        [rows_ref[:, g * HD : (g + 1) * HD] for g in range(group)], 0
    )
    count = span * group
    scale = HD**-0.5
    token = lax.broadcasted_iota(jnp.int32, (count, 1), 0) % span
    oldest = jnp.maximum(token + 1, cycle - length + 4)
    wide[...] = sink_ref[seq].astype(F32)
    pad = jnp.zeros((span - 4, HD), F32)
    first_k = jnp.concatenate(
        [
            jnp.concatenate([wide[pl.ds(0, 4, stride=2), :], pad], 0).astype(BF),
            rows_ref[:, 4 * HD : 5 * HD],
        ],
        0,
    )
    first_v = jnp.concatenate(
        [
            jnp.concatenate([wide[pl.ds(1, 4, stride=2), :], pad], 0).astype(BF),
            rows_ref[:, 5 * HD : 6 * HD],
        ],
        0,
    )
    column = lax.broadcasted_iota(jnp.int32, (1, 2 * span), 1)
    live = (column < 4) | ((column >= span) & (column - span <= token))
    low = jnp.float32(-jnp.inf)
    first = jnp.where(live, dot_t(query, first_k), low)
    peak = first
    for n in range(cycle // CHUNK):
        part = dot_t(query, k_ref[n * CHUNK : (n + 1) * CHUNK, :])
        age = lax.broadcasted_iota(jnp.int32, (1, CHUNK), 1) + (n * CHUNK - offset)
        age = jnp.where(age < 0, age + cycle, age)
        part = jnp.where(age >= oldest, part, low)
        scores[:, n * CHUNK : (n + 1) * CHUNK] = part
        for m in range(CHUNK // HD):
            peak = jnp.maximum(peak, part[:, m * HD : (m + 1) * HD])
    top = jnp.max(peak, 1, keepdims=True)
    expo = jnp.exp((first - top) * scale)
    total = expo
    acc = dot(expo.astype(BF), first_v)
    for n in range(cycle // CHUNK):
        expo = jnp.exp((scores[:, n * CHUNK : (n + 1) * CHUNK] - top) * scale)
        for m in range(CHUNK // HD):
            total = total + expo[:, m * HD : (m + 1) * HD]
        acc = acc + dot(expo.astype(BF), v_ref[n * CHUNK : (n + 1) * CHUNK, :])
    mixed = acc / jnp.sum(total, 1, keepdims=True)
    for g in range(group):
        out_ref[:, g * HD : (g + 1) * HD] = mixed[g * span : (g + 1) * span].astype(BF)


def write_body(seq_ref, off_ref, rows_ref, cache_ref, out_ref):
    offset = off_ref[seq_ref[0]]
    step = cache_ref.shape[0]
    span = rows_ref.shape[0]
    cycle = step * pl.num_programs(0) // 2
    row = lax.broadcasted_iota(jnp.int32, (step, 1), 0) + pl.program_id(0) * step
    age = row // 2 - offset
    age = jnp.where(age < 0, age + cycle, age)
    column = lax.broadcasted_iota(jnp.int32, (1, 2 * span), 1)
    hot = jnp.where(age + (row % 2) * span == column, 1.0, 0.0)
    hot = jnp.where(age < span, hot, 0.0).astype(BF)
    new = jnp.concatenate(
        [rows_ref[:, 4 * HD : 5 * HD], rows_ref[:, 5 * HD : 6 * HD]], 0
    )
    fresh = dot(hot, new)
    out_ref[...] = jnp.where(age < span, fresh, cache_ref[...].astype(F32)).astype(BF)


def write_cycle(seq, offsets, rows, cache_rows):
    total, step = cache_rows.shape[0], 1024
    return pl.pallas_call(
        write_body,
        grid=(total // step,),
        out_shape=shape(total, HD),
        in_specs=[
            SMEM,
            SMEM,
            pl.BlockSpec(rows.shape, lambda n: (0, 0)),
            pl.BlockSpec((step, HD), lambda n: (n, 0)),
        ],
        out_specs=pl.BlockSpec((step, HD), lambda n: (n, 0)),
        cost_estimate=pl.CostEstimate(
            flops=1 << 28, bytes_accessed=8 << 20, transcendentals=0
        ),
        name="write_cycle",
    )(seq, offsets, rows, cache_rows)


def project_body(core_ref, own_ref, other_ref, w_ref, out_ref):
    first = core_ref[0] == 0
    own, other = own_ref[...], other_ref[...]
    rows = own.shape[0]
    own32, other32 = own.astype(F32), other.astype(F32)
    both = jnp.concatenate(
        [jnp.where(first, own32, other32), jnp.where(first, other32, own32)], 0
    ).astype(BF)
    weight = jnp.concatenate([w_ref[0, 0], w_ref[1, 0]], 1)
    result = dot(both, weight).astype(BF)
    out_ref[0, 0] = result[:rows]
    out_ref[1, 0] = result[rows:]


def project(core, own, other, weight):
    rows = own.shape[0]
    return pl.pallas_call(
        project_body,
        grid=(8,),
        out_shape=shape(2, 8, rows, 256),
        in_specs=[
            SMEM,
            pl.BlockSpec(own.shape, lambda h: (0, 0)),
            pl.BlockSpec(own.shape, lambda h: (0, 0)),
            pl.BlockSpec((2, 1, 512, 128), lambda h: (h % 4, h // 4, 0, 0)),
        ],
        out_specs=pl.BlockSpec((2, 1, rows, 256), lambda h: (0, h, 0, 0)),
        cost_estimate=pl.CostEstimate(
            flops=1 << 28, bytes_accessed=3 << 20, transcendentals=0
        ),
        name="project",
    )(core, own, other, weight)


def pieces(value):
    high = value.astype(BF).astype(F32)
    rest = value - high
    middle = rest.astype(BF).astype(F32)
    return high, middle, (rest - middle).astype(BF).astype(F32)


def dispatch_body(
    order_ref,
    part_ref,
    res_ref,
    gain_ref,
    router_ref,
    ids_ref,
    ids_t_ref,
    hidden_ref,
    code_ref,
    send_ref,
):
    hot = jnp.where(slot_of_request(order_ref[...]), 1.0, 0.0).astype(BF)
    resid = jnp.concatenate([dot(hot, res_ref[i]) for i in range(2)], 0)
    picks = jnp.concatenate(
        [dot(hot, ids_ref[i].astype(F32).astype(BF)) for i in range(2)], 0
    )
    picks_t = jnp.concatenate(
        [dot_t(ids_t_ref[i].astype(F32).astype(BF), hot) for i in range(2)], 1
    )
    sums = []
    for c in range(2):
        total = part_ref[c * 8].astype(F32)
        for h in range(1, 8):
            total = total + part_ref[c * 8 + h].astype(F32)
        sums.append(total)
    projected = jnp.concatenate(
        [sums[0][:, :HD], sums[1][:, :HD], sums[0][:, HD:], sums[1][:, HD:]], 1
    )
    hidden = resid + projected
    hidden_ref[...] = hidden
    gained = hidden * gain_ref[...]
    square = jnp.sum(hidden * hidden, 1, keepdims=True)
    share = jnp.dot(
        gained,
        router_ref[...],
        precision=lax.Precision.HIGHEST,
        preferred_element_type=F32,
    )
    rows = hidden.shape[0]
    one, two = picks[:, 0:1], picks[:, 1:2]
    expert = lax.broadcasted_iota(jnp.int32, (1, E), 1).astype(F32)
    first, second = one == expert, two == expert
    apart = jnp.sum(jnp.where(first, share, 0.0) - jnp.where(second, share, 0.0), 1, keepdims=True)
    before = lax.broadcasted_iota(jnp.int32, (rows, rows), 0)
    after = lax.broadcasted_iota(jnp.int32, (rows, rows), 1)
    lower = jnp.where(before > after, 1.0, 0.0).astype(BF)
    upper = jnp.where(before < after, 1.0, 0.0).astype(BF)
    earlier = dot(lower, jnp.where(first | second, 1.0, 0.0).astype(BF))
    slot_one = jnp.sum(jnp.where(first, earlier, 0.0), 1, keepdims=True)
    slot_two = jnp.sum(jnp.where(second, earlier, 0.0), 1, keepdims=True)
    lane = lax.broadcasted_iota(jnp.int32, (rows, HD), 1)
    code_ref[...] = jnp.where(
        lane == 0, one * SLOT + slot_one, two * SLOT + slot_two
    ).astype(jnp.int32)
    one_t, two_t = picks_t[0:1], picks_t[1:2]
    expert_t = lax.broadcasted_iota(jnp.int32, (E, 1), 0).astype(F32)
    first_t, second_t = one_t == expert_t, two_t == expert_t
    earlier_t = dot(jnp.where(first_t | second_t, 1.0, 0.0).astype(BF), upper)
    slot_one_t = jnp.sum(jnp.where(first_t, earlier_t, 0.0), 0, keepdims=True)
    slot_two_t = jnp.sum(jnp.where(second_t, earlier_t, 0.0), 0, keepdims=True)
    place = lax.broadcasted_iota(jnp.int32, (E * SLOT, 1), 0).astype(F32)
    is_one = jnp.where(place == one_t * SLOT + slot_one_t, 1.0, 0.0)
    is_two = jnp.where(place == two_t * SLOT + slot_two_t, 1.0, 0.0)
    plus, minus = (is_one + is_two).astype(BF), (is_one - is_two).astype(BF)
    bucket = dot(plus, gained.astype(BF)).astype(BF)
    norm_terms, gate_terms = jnp.zeros((rows, HD), F32), jnp.zeros((rows, HD), F32)
    for n, (s, a) in enumerate(zip(pieces(square), pieces(apart))):
        norm_terms = jnp.where(lane == n, s, norm_terms)
        gate_terms = jnp.where(lane == 3 + n, a, gate_terms)
    terms = (dot(plus, norm_terms.astype(BF)) + dot(minus, gate_terms.astype(BF))).astype(BF)
    for e in range(E):
        for x in range(2):
            send_ref[x * E + e, :, 0:512] = bucket[e * SLOT : e * SLOT + CAP]
            send_ref[x * E + e, :, 512:640] = terms[e * SLOT : e * SLOT + CAP]


def norm_body(got_ref, x_ref, gate_ref):
    target = lax.broadcasted_iota(jnp.int32, (2 * CAP, CAP), 0)
    source = lax.broadcasted_iota(jnp.int32, (2 * CAP, CAP), 1)
    put = [jnp.where(target == source + CAP * x, 1.0, 0.0).astype(BF) for x in range(2)]
    terms = jnp.zeros((2 * CAP, HD), F32)
    for h in range(8):
        for x in range(2):
            terms = terms + dot(put[x], got_ref[x * 8 + h, :, 512:640])
    lane = lax.broadcasted_iota(jnp.int32, (2 * CAP, HD), 1)
    square = jnp.sum(jnp.where(lane < 3, terms, 0.0), 1, keepdims=True)
    apart = jnp.sum(jnp.where((lane >= 3) & (lane < 6), terms, 0.0), 1, keepdims=True)
    inv_rms = lax.rsqrt(square / D + 1e-05)
    gate = 1.0 / (1.0 + jnp.exp(-(apart * inv_rms)))
    gate_ref[...] = jnp.broadcast_to(gate.astype(BF).astype(F32), gate_ref.shape)
    for h in range(8):
        part = dot(put[0], got_ref[h, :, 0:512]) + dot(put[1], got_ref[8 + h, :, 0:512])
        x_ref[:, h * 512 : (h + 1) * 512] = (part * inv_rms).astype(BF)


ROWS = 2 * CAP
PAD = 48


def expert_body(*refs):
    x_refs, refs = refs[:9], refs[9:]
    own_ref, other_ref, down_ref, other_down_ref = refs[:4]
    out_refs, (x, inner) = refs[4:13], refs[13:]
    step = pl.program_id(0)

    @pl.when(step == 0)
    def _():
        for n in range(7):
            x[n * PAD : n * PAD + ROWS, :] = x_refs[n][...]
        x[7 * PAD : 7 * PAD + ROWS, : D // 2] = x_refs[7][...]
        x[7 * PAD : 7 * PAD + ROWS, D // 2 :] = x_refs[8][...]

    for n, w_ref in ((0, own_ref), (1, other_ref)):

        @pl.when(step == n)
        def _(n=n, w_ref=w_ref):
            gate, up = dot(x[...], w_ref[0]), dot(x[...], w_ref[1])
            inner[:, n * 256 : (n + 1) * 256] = (
                gate / (1.0 + jnp.exp(-gate)) * up
            ).astype(BF)

    @pl.when(step >= 2)
    def _():
        result = dot(inner[:, :256], down_ref[...]) + dot(inner[:, 256:], other_down_ref[...])
        result = result.astype(BF)
        for n in range(7):
            out_refs[n][...] = result[n * PAD : n * PAD + ROWS]
        last = result[7 * PAD : 7 * PAD + ROWS]

        @pl.when(step < 4)
        def _():
            out_refs[7][...] = last

        @pl.when(step >= 4)
        def _():
            out_refs[8][...] = last


def expert(blocks, own, other, down, other_down):
    width = 1024
    column = lambda j: (0, jnp.maximum(j - 2, 0))
    left = lambda j: (0, jnp.clip(j - 2, 0, 1))
    right = lambda j: (0, jnp.maximum(j - 4, 0))
    whole = lambda a: pl.BlockSpec(a.shape, lambda j: (0,) * a.ndim)
    wide = pl.BlockSpec((ROWS, width), column)
    return pl.pallas_call(
        expert_body,
        grid=(6,),
        out_shape=[shape(ROWS, D)] * 7 + [shape(ROWS, D // 2)] * 2,
        in_specs=[whole(b) for b in blocks]
        + [whole(own), whole(other)]
        + [pl.BlockSpec((256, width), column)] * 2,
        out_specs=[wide] * 7
        + [pl.BlockSpec((ROWS, width), left), pl.BlockSpec((ROWS, width), right)],
        scratch_shapes=[pltpu.VMEM((8 * PAD, D), BF), pltpu.VMEM((8 * PAD, 512), BF)],
        compiler_params=pltpu.CompilerParams(vmem_limit_bytes=48 << 20),
        cost_estimate=pl.CostEstimate(
            flops=4 << 30, bytes_accessed=18 << 20, transcendentals=0
        ),
        name="expert",
    )(*blocks, own, other, down, other_down)


def gate_body(own_ref, right_ref, left_ref, gate_ref, send_ref):
    target = lax.broadcasted_iota(jnp.int32, (CAP, ROWS), 0)
    source = lax.broadcasted_iota(jnp.int32, (CAP, ROWS), 1)
    take = [jnp.where(target + CAP * x == source, 1.0, 0.0).astype(BF) for x in range(2)]
    for h in range(8):
        cut = slice(h * 512, (h + 1) * 512)
        total = own_ref[:, cut].astype(F32) + right_ref[:, cut].astype(F32)
        total = (total + left_ref[:, cut].astype(F32)) * gate_ref[:, 0:1]
        total = total.astype(BF)
        for x in range(2):
            send_ref[x * 8 + h] = dot(take[x], total).astype(BF)


def combine_body(hidden_ref, code_ref, got_ref, out_ref):
    total = hidden_ref[...]
    rows = total.shape[0]
    one, two = code_ref[:, 0:1], code_ref[:, 1:2]
    lane = lax.broadcasted_iota(jnp.int32, (rows, CAP), 1)
    for e in range(E):
        at = lane + e * SLOT
        hot = jnp.where((one == at) | (two == at), 1.0, 0.0).astype(BF)
        total = total + dot(hot, got_ref[e]) + dot(hot, got_ref[8 + e])
    out_ref[0] = total[: rows // 2].astype(BF)
    out_ref[1] = total[rows // 2 :].astype(BF)


def shards(
    queries,
    new_kv,
    cache,
    sinks,
    lengths,
    offsets,
    order,
    residual,
    o_weight,
    ffn_gain,
    router,
    expert_ids,
    w_in,
    w_out,
):
    seq = lax.axis_index(SEQ).astype(jnp.int32).reshape(1)
    core = lax.axis_index("c").astype(jnp.int32).reshape(1)
    swap = [(0, 1), (1, 0)]
    right = [(i, (i + 1) % NZ) for i in range(NZ)]
    left = [(i, (i - 1) % NZ) for i in range(NZ)]
    order_row = order.reshape(1, -1)

    o_other = lax.ppermute(o_weight, "xh", swap)
    low = lax.axis_index("xh") == 0
    o_pair = jnp.stack(
        [jnp.where(low, o_weight, o_other), jnp.where(low, o_other, o_weight)], 0
    )
    o_all = lax.all_gather(o_pair, "z", axis=0, tiled=False)

    kv = new_kv.reshape(2, 32, 256)
    asked = call(permute_body, shape(2, 32, 768), "permute", 3)(order_row, queries, kv)
    rows = lax.all_to_all(asked, SEQ, split_axis=1, concat_axis=0, tiled=True)
    rows = rows.reshape(64, 768)

    cache_rows = cache.reshape(8192, HD)
    keys, values = split_cycle(cache_rows)
    attended = call(
        attend_body,
        shape(64, 512),
        "attend",
        7,
        scalars=3,
        flops=1 << 30,
        nbytes=2 << 20,
        scratch=[pltpu.VMEM((256, 4096), F32), pltpu.VMEM((8, HD), F32)],
    )(seq, lengths, offsets, rows, keys, values, sinks.reshape(32, 8, HD))
    cache_out = write_cycle(seq, offsets, rows, cache_rows).reshape(cache.shape)

    w_in, w_out = w_in[0], w_out[0]
    w_in_other = lax.ppermute(w_in, "c", swap)
    w_out_other = lax.ppermute(w_out, "c", swap)
    w_own, w_other = w_in.transpose(1, 0, 2), w_in_other.transpose(1, 0, 2)

    owned = lax.all_to_all(
        attended.reshape(64, 1, 512), SEQ, split_axis=0, concat_axis=1, tiled=True
    )
    owned = owned.reshape(64, 512)
    owned_other = lax.ppermute(owned, "c", swap)
    share = project(core, owned, owned_other, o_all)
    share = lax.all_to_all(
        share.reshape(16, 64, 256), ("c",) + HEAD, split_axis=0, concat_axis=0, tiled=True
    )
    ids_t = expert_ids.transpose(0, 2, 1)
    hidden, codes, send = call(
        dispatch_body,
        [shape(64, 512, dtype=F32), shape(64, HD, dtype=jnp.int32), shape(16, CAP, 640)],
        "dispatch",
        7,
        flops=1 << 26,
        nbytes=2 << 20,
    )(order_row, share, residual, ffn_gain.reshape(1, -1), router, expert_ids, ids_t)
    got = lax.all_to_all(send, ("xh",) + HEAD, split_axis=0, concat_axis=0, tiled=True)
    x, gate = call(
        norm_body,
        [shape(ROWS, D), shape(ROWS, HD, dtype=F32)],
        "norm",
        1,
        flops=1 << 26,
        nbytes=1 << 20,
    )(got)

    from_left, from_right = [x], [x]
    for _ in range(3):
        from_left.append(lax.ppermute(from_left[-1], "z", right))
        from_right.append(lax.ppermute(from_right[-1], "z", left))
    far_left = lax.ppermute(from_left[3][:, : D // 2], "z", right)
    far_right = lax.ppermute(from_right[3][:, D // 2 :], "z", left)
    blocks = [x] + from_left[1:] + from_right[1:] + [far_left, far_right]
    parts = expert(blocks, w_own, w_other, w_out, w_out_other)
    own, at_left, at_right = parts[0], parts[1:4], parts[4:7]

    def add(a, b):
        return (a.astype(F32) + b.astype(F32)).astype(BF)

    half = D // 2
    to_right = lax.ppermute(parts[7], "z", right)
    to_left = lax.ppermute(parts[8], "z", left)
    to_right = jnp.concatenate(
        [add(at_right[2][:, :half], to_right), at_right[2][:, half:]], 1
    )
    to_left = jnp.concatenate(
        [at_left[2][:, :half], add(at_left[2][:, half:], to_left)], 1
    )
    for n in (1, 0):
        to_right = add(at_right[n], lax.ppermute(to_right, "z", right))
        to_left = add(at_left[n], lax.ppermute(to_left, "z", left))
    to_right = lax.ppermute(to_right, "z", right)
    to_left = lax.ppermute(to_left, "z", left)
    back = call(gate_body, shape(16, CAP, 512), "gate", 4, flops=1 << 26, nbytes=2 << 20)(
        own, to_right, to_left, gate
    )
    back = lax.all_to_all(back, ("xh",) + HEAD, split_axis=0, concat_axis=0, tiled=True)
    layer_out = call(
        combine_body, shape(2, 32, 512), "combine", 3, flops=1 << 26, nbytes=1 << 20
    )(hidden, codes, back)
    return (layer_out, cache_out)


def solution(mesh):
    fine = Mesh(mesh.devices.reshape(2, NZ, 2, 2, 4), SEQ + HEAD)
    return jax.shard_map(
        shards,
        mesh=fine,
        in_specs=(
            P(SEQ, None, HEAD),
            P(SEQ, None, None, HEAD),
            P(SEQ, None, None, HEAD),
            P(None, None, None, HEAD),
            P(),
            P(),
            P(),
            P(SEQ, None, HEAD),
            P(HEAD, SEQ),
            P(HEAD),
            P(HEAD, None),
            P(SEQ, None, None),
            P(HEAD, None, None, SEQ),
            P(HEAD, SEQ, None),
        ),
        out_specs=(P(SEQ, None, HEAD), P(SEQ, None, None, HEAD)),
        check_vma=False,
    )
```

```python
import functools

import jax
import jax.numpy as jnp
from jax import lax
from jax.experimental import pallas as pl
from jax.experimental.pallas import tpu as pltpu
from jax.sharding import Mesh
from jax.sharding import PartitionSpec as P

D = 4096
HD = 128
E = 8
CAP = 18
SLOT = 24
NZ = 8
BF = jnp.bfloat16
F32 = jnp.float32
VMEM = pl.BlockSpec(memory_space=pltpu.VMEM)
ANY = pl.BlockSpec(memory_space=pl.ANY)
HBM = pl.BlockSpec(memory_space=pltpu.HBM)
SMEM = pl.BlockSpec(memory_space=pltpu.SMEM)
SEQ = ("xh", "z", "c")
HEAD = ("xl", "y")


def call(
    body, outs, name, n_in, scalars=0, after=0, flops=0, nbytes=0, limit=20, scratch=(), keep=False
):
    return pl.pallas_call(
        body,
        out_shape=outs,
        in_specs=[SMEM] * scalars
        + [VMEM] * (n_in - scalars)
        + [HBM if keep else ANY] * after,
        out_specs=[VMEM] * (len(outs) - 1) + [HBM]
        if keep
        else jax.tree.map(lambda _: VMEM, outs),
        input_output_aliases={n_in + after - 1: len(outs) - 1} if keep else {},
        scratch_shapes=list(scratch),
        compiler_params=pltpu.CompilerParams(vmem_limit_bytes=limit << 20),
        cost_estimate=pl.CostEstimate(
            flops=flops, bytes_accessed=nbytes, transcendentals=0
        ),
        name=name,
    )


def shape(*dims, dtype=BF):
    return jax.ShapeDtypeStruct(dims, dtype)


def dot(a, b):
    return jnp.dot(a, b, preferred_element_type=F32)


def dot_t(a, b):
    return lax.dot_general(a, b, (((1,), (1,)), ((), ())), preferred_element_type=F32)


def slot_of_request(order_row):
    n = order_row.shape[1]
    return order_row == lax.broadcasted_iota(jnp.int32, (n, n), 0)


ASK = 16


def permute_body(order_ref, q_ref, kv_ref, out_ref, wide):
    hot = jnp.where(slot_of_request(order_ref[...]), 1.0, 0.0).astype(BF)
    count = hot.shape[0]
    wide[...] = jnp.zeros_like(wide)
    for i in range(2):
        rows = jnp.concatenate([q_ref[i], kv_ref[i, :, 0, :], kv_ref[i, :, 1, :]], 1)
        rows = dot(hot, rows)
        for g in range(6):
            wide[pl.ds(i * 6 + g, count, stride=ASK), :] = rows[:, g * HD : (g + 1) * HD]
    out_ref[...] = wide[...].astype(BF)


def split_body(cache_ref, k_ref, v_ref, wide):
    rows = cache_ref.shape[0]
    wide[...] = cache_ref[...].astype(F32)
    k_ref[...] = wide[pl.ds(0, rows // 2, stride=2), :].astype(BF)
    v_ref[...] = wide[pl.ds(1, rows // 2, stride=2), :].astype(BF)


def split_cycle(cache_rows):
    rows = cache_rows.shape[0]
    return call(
        split_body,
        [shape(rows // 2, HD)] * 2,
        "split_cycle",
        1,
        flops=1 << 24,
        nbytes=8 << 20,
        scratch=[pltpu.VMEM((rows, HD), F32)],
    )(cache_rows)


CHUNK = 512


def attend_body(
    seq_ref,
    len_ref,
    off_ref,
    rows_ref,
    sink_ref,
    k_ref,
    v_ref,
    weight_ref,
    out_ref,
    new_ref,
    weight_out_ref,
    scores,
    wide,
    asked,
    mixed_rows,
):
    seq = seq_ref[0]
    length, offset = len_ref[seq], off_ref[seq]
    half = rows_ref.shape[0] // ASK
    span = 2 * half
    cycle = k_ref.shape[0]
    group = 4
    asked[...] = rows_ref[...].astype(F32)

    def piece(g):
        return jnp.concatenate(
            [asked[pl.ds(i * 6 + g, half, stride=ASK), :] for i in range(2)], 0
        )

    query = jnp.concatenate([piece(g) for g in range(group)], 0).astype(BF)
    new_k, new_v = piece(4), piece(5)
    new_ref[...] = jnp.concatenate([new_k, new_v], 0).astype(BF)
    count = span * group
    scale = HD**-0.5
    row = lax.broadcasted_iota(jnp.int32, (count, 1), 0) % span
    token = row % half * 2 + row // half
    oldest = jnp.maximum(token + 1, cycle - length + 4)
    wide[...] = sink_ref[seq].astype(F32)
    pad = jnp.zeros((span - 4, HD), F32)
    first_k = jnp.concatenate([wide[pl.ds(0, 4, stride=2), :], pad, new_k], 0).astype(BF)
    first_v = jnp.concatenate([wide[pl.ds(1, 4, stride=2), :], pad, new_v], 0).astype(BF)
    column = lax.broadcasted_iota(jnp.int32, (1, 2 * span), 1)
    at = column - span
    live = (column < 4) | ((at >= 0) & (at % half * 2 + at // half <= token))
    low = jnp.float32(-jnp.inf)
    first = jnp.where(live, dot_t(query, first_k), low)
    peak = first
    for n in range(cycle // CHUNK):
        part = dot_t(query, k_ref[n * CHUNK : (n + 1) * CHUNK, :])
        age = lax.broadcasted_iota(jnp.int32, (1, CHUNK), 1) + (n * CHUNK - offset)
        age = jnp.where(age < 0, age + cycle, age)
        part = jnp.where(age >= oldest, part, low)
        scores[:, n * CHUNK : (n + 1) * CHUNK] = part
        for m in range(CHUNK // HD):
            peak = jnp.maximum(peak, part[:, m * HD : (m + 1) * HD])
    top = jnp.max(peak, 1, keepdims=True)
    expo = jnp.exp((first - top) * scale)
    total = expo
    acc = dot(expo.astype(BF), first_v)
    for n in range(cycle // CHUNK):
        expo = jnp.exp((scores[:, n * CHUNK : (n + 1) * CHUNK] - top) * scale)
        for m in range(CHUNK // HD):
            total = total + expo[:, m * HD : (m + 1) * HD]
        acc = acc + dot(expo.astype(BF), v_ref[n * CHUNK : (n + 1) * CHUNK, :])
    mixed = acc / jnp.sum(total, 1, keepdims=True)
    for g in range(group):
        for i in range(2):
            first_row = g * span + i * half
            mixed_rows[pl.ds(i * 4 + g, half, stride=8), :] = mixed[
                first_row : first_row + half
            ]
    out_ref[...] = mixed_rows[...].astype(BF)


WINDOW = 144


def write_body(seq_ref, off_ref, new_ref, cache_ref, after_ref, out_ref, done_ref):
    done_ref[...] = jnp.zeros_like(done_ref)
    offset = off_ref[seq_ref[0]]
    step = cache_ref.shape[0]
    total = step * pl.num_programs(0)
    span = new_ref.shape[0] // 2
    half = span // 2
    out_ref[...] = cache_ref[...]
    for wrap in (0, 1):
        first = 2 * offset - wrap * total - pl.program_id(0) * step

        @pl.when((first > -2 * span) & (first < step))
        def _(first=first):
            start = jnp.clip(first, 0, step - WINDOW) // 16 * 16
            window = pl.ds(pl.multiple_of(start, 16), WINDOW)
            row = lax.broadcasted_iota(jnp.int32, (WINDOW, 1), 0) + start
            at = row - first
            column = lax.broadcasted_iota(jnp.int32, (1, 2 * span), 1)
            hot = at % 2 * span + at // 2 % 2 * half + at // 4 == column
            written = (at >= 0) & (at < 2 * span)
            hot = jnp.where(written & hot, 1.0, 0.0).astype(BF)
            fresh = dot(hot, new_ref[...])
            old = out_ref[window, :].astype(F32)
            out_ref[window, :] = jnp.where(written, fresh, old).astype(BF)


def write_cycle(seq, offsets, new, cache_rows, after):
    total, step = cache_rows.shape[0], 2048
    return pl.pallas_call(
        write_body,
        grid=(total // step,),
        out_shape=[shape(total, HD), shape(8, HD, dtype=F32)],
        in_specs=[
            SMEM,
            SMEM,
            pl.BlockSpec(new.shape, lambda n: (0, 0)),
            pl.BlockSpec((step, HD), lambda n: (n, 0)),
            ANY,
        ],
        out_specs=[
            pl.BlockSpec((step, HD), lambda n: (n, 0)),
            pl.BlockSpec((8, HD), lambda n: (0, 0)),
        ],
        cost_estimate=pl.CostEstimate(
            flops=1 << 24, bytes_accessed=16 << 20, transcendentals=0
        ),
        compiler_params=pltpu.CompilerParams(vmem_limit_bytes=16 << 20),
        name="write_cycle",
    )(seq, offsets, new, cache_rows, after)


def pair_body(xh_ref, own_ref, other_ref, after_ref, out_ref):
    xh = xh_ref[0]
    out_ref[xh] = own_ref[...]
    out_ref[1 - xh] = other_ref[...]


def unmix_body(w_ref, after_ref, out_ref):
    for k in range(2):
        out_ref[k] = w_ref[:, k, :]


def unmix(w_in, after):
    step = 512
    return pl.pallas_call(
        unmix_body,
        grid=(D // step,),
        out_shape=shape(2, D, 256),
        in_specs=[pl.BlockSpec((step, 2, 256), lambda n: (n, 0, 0)), ANY],
        out_specs=pl.BlockSpec((2, step, 256), lambda n: (0, n, 0)),
        cost_estimate=pl.CostEstimate(
            flops=1 << 20, bytes_accessed=16 << 20, transcendentals=0
        ),
        compiler_params=pltpu.CompilerParams(vmem_limit_bytes=16 << 20),
        name="unmix",
    )(w_in, after)


def project_body(core_ref, own_ref, other_ref, w_ref, out_ref, wide, both):
    half = own_ref.shape[0] // 8
    rows = 2 * half

    @pl.when(pl.program_id(0) == 0)
    def _():
        first = core_ref[0] == 0
        own, other = own_ref[...].astype(F32), other_ref[...].astype(F32)
        for c in range(2):
            wide[...] = jnp.where(first == (c == 0), own, other)
            for i in range(2):
                for g in range(4):
                    at = c * rows + i * half
                    both[at : at + half, g * HD : (g + 1) * HD] = wide[
                        pl.ds(i * 4 + g, half, stride=8), :
                    ].astype(BF)

    for n in range(2):
        weight = jnp.concatenate([w_ref[2 * n, 0], w_ref[2 * n + 1, 0]], 1)
        result = dot(both[...], weight).astype(BF)
        out_ref[0, n] = result[:rows]
        out_ref[1, n] = result[rows:]


def project(core, own, other, weight):
    rows = own.shape[0] // 4
    return pl.pallas_call(
        project_body,
        grid=(4,),
        out_shape=shape(2, 8, rows, 256),
        in_specs=[
            SMEM,
            pl.BlockSpec(own.shape, lambda n: (0, 0)),
            pl.BlockSpec(own.shape, lambda n: (0, 0)),
            pl.BlockSpec((4, 1, 512, 128), lambda n: (n % 2, n // 2, 0, 0)),
        ],
        out_specs=pl.BlockSpec((2, 2, rows, 256), lambda n: (0, n, 0, 0)),
        scratch_shapes=[pltpu.VMEM(own.shape, F32), pltpu.VMEM((2 * rows, 512), BF)],
        cost_estimate=pl.CostEstimate(
            flops=1 << 28, bytes_accessed=3 << 20, transcendentals=0
        ),
        compiler_params=pltpu.CompilerParams(vmem_limit_bytes=16 << 20),
        name="project",
    )(core, own, other, weight)


def pieces(value):
    high = value.astype(BF).astype(F32)
    rest = value - high
    middle = rest.astype(BF).astype(F32)
    return high, middle, (rest - middle).astype(BF).astype(F32)


def dispatch_body(
    order_ref,
    part_ref,
    res_ref,
    gain_ref,
    router_ref,
    ids_ref,
    ids_t_ref,
    hidden_ref,
    code_ref,
    send_ref,
):
    hot = jnp.where(slot_of_request(order_ref[...]), 1.0, 0.0).astype(BF)
    resid = jnp.concatenate([dot(hot, res_ref[i]) for i in range(2)], 0)
    picks = jnp.concatenate(
        [dot(hot, ids_ref[i].astype(F32).astype(BF)) for i in range(2)], 0
    )
    picks_t = jnp.concatenate(
        [dot_t(ids_t_ref[i].astype(F32).astype(BF), hot) for i in range(2)], 1
    )
    sums = []
    for c in range(2):
        total = part_ref[c * 8].astype(F32)
        for h in range(1, 8):
            total = total + part_ref[c * 8 + h].astype(F32)
        sums.append(total)
    projected = jnp.concatenate(
        [sums[0][:, :HD], sums[1][:, :HD], sums[0][:, HD:], sums[1][:, HD:]], 1
    )
    hidden = resid + projected
    hidden_ref[...] = hidden
    gained = hidden * gain_ref[...]
    square = jnp.sum(hidden * hidden, 1, keepdims=True)
    share = jnp.dot(
        gained,
        router_ref[...],
        precision=lax.Precision.HIGHEST,
        preferred_element_type=F32,
    )
    rows = hidden.shape[0]
    one, two = picks[:, 0:1], picks[:, 1:2]
    expert = lax.broadcasted_iota(jnp.int32, (1, E), 1).astype(F32)
    first, second = one == expert, two == expert
    apart = jnp.sum(jnp.where(first, share, 0.0) - jnp.where(second, share, 0.0), 1, keepdims=True)
    before = lax.broadcasted_iota(jnp.int32, (rows, rows), 0)
    after = lax.broadcasted_iota(jnp.int32, (rows, rows), 1)
    lower = jnp.where(before > after, 1.0, 0.0).astype(BF)
    upper = jnp.where(before < after, 1.0, 0.0).astype(BF)
    earlier = dot(lower, jnp.where(first | second, 1.0, 0.0).astype(BF))
    slot_one = jnp.sum(jnp.where(first, earlier, 0.0), 1, keepdims=True)
    slot_two = jnp.sum(jnp.where(second, earlier, 0.0), 1, keepdims=True)
    lane = lax.broadcasted_iota(jnp.int32, (rows, HD), 1)
    code_ref[...] = jnp.where(
        lane == 0, one * SLOT + slot_one, two * SLOT + slot_two
    ).astype(jnp.int32)
    one_t, two_t = picks_t[0:1], picks_t[1:2]
    expert_t = lax.broadcasted_iota(jnp.int32, (E, 1), 0).astype(F32)
    first_t, second_t = one_t == expert_t, two_t == expert_t
    earlier_t = dot(jnp.where(first_t | second_t, 1.0, 0.0).astype(BF), upper)
    slot_one_t = jnp.sum(jnp.where(first_t, earlier_t, 0.0), 0, keepdims=True)
    slot_two_t = jnp.sum(jnp.where(second_t, earlier_t, 0.0), 0, keepdims=True)
    place = lax.broadcasted_iota(jnp.int32, (E * SLOT, 1), 0).astype(F32)
    is_one = jnp.where(place == one_t * SLOT + slot_one_t, 1.0, 0.0)
    is_two = jnp.where(place == two_t * SLOT + slot_two_t, 1.0, 0.0)
    plus, minus = (is_one + is_two).astype(BF), (is_one - is_two).astype(BF)
    bucket = dot(plus, gained.astype(BF)).astype(BF)
    norm_terms, gate_terms = jnp.zeros((rows, HD), F32), jnp.zeros((rows, HD), F32)
    for n, (s, a) in enumerate(zip(pieces(square), pieces(apart))):
        norm_terms = jnp.where(lane == n, s, norm_terms)
        gate_terms = jnp.where(lane == 3 + n, a, gate_terms)
    terms = (dot(plus, norm_terms.astype(BF)) + dot(minus, gate_terms.astype(BF))).astype(BF)
    for e in range(E):
        for x in range(2):
            send_ref[x * E + e, :, 0:512] = bucket[e * SLOT : e * SLOT + CAP]
            send_ref[x * E + e, :, 512:640] = terms[e * SLOT : e * SLOT + CAP]


QUARTER = D // 4
BLOCK = 8 * CAP


def norm_body(got_ref, after_ref, x_ref, gate_ref):
    target = lax.broadcasted_iota(jnp.int32, (BLOCK, CAP), 0)
    source = lax.broadcasted_iota(jnp.int32, (BLOCK, CAP), 1)
    lane = lax.broadcasted_iota(jnp.int32, (CAP, HD), 1)
    parts, gates = [0.0, 0.0], 0.0
    for x in range(2):
        terms = got_ref[x * 8, :, 512:640].astype(F32)
        for h in range(1, 8):
            terms = terms + got_ref[x * 8 + h, :, 512:640].astype(F32)
        square = jnp.sum(jnp.where(lane < 3, terms, 0.0), 1, keepdims=True)
        apart = jnp.sum(jnp.where((lane >= 3) & (lane < 6), terms, 0.0), 1, keepdims=True)
        inv_rms = lax.rsqrt(square / D + 1e-05)
        gate = 1.0 / (1.0 + jnp.exp(-(apart * inv_rms)))
        gate = jnp.broadcast_to(gate, (CAP, HD)).astype(BF)
        for q in range(4):
            put = jnp.where(target == source + CAP * (4 * x + q), 1.0, 0.0).astype(BF)
            gates = gates + dot(put, gate)
            for n in range(2):
                rows = got_ref[x * 8 + 2 * q + n, :, 0:512].astype(F32) * inv_rms
                parts[n] = parts[n] + dot(put, rows.astype(BF))
    gate_ref[...] = gates
    for n in range(2):
        x_ref[:, n * 512 : (n + 1) * 512] = parts[n].astype(BF)


def expert_body(*refs):
    x_refs, refs = refs[:9], refs[9:]
    w_refs, down_refs = refs[0:2], refs[2:4]
    out_refs, (x, sums, inner) = refs[4:12], refs[12:]
    half = QUARTER // 2
    step = pl.program_id(0)
    for q in range(4):

        @pl.when(step == q)
        def _(q=q):
            for n in range(8):
                for b in range(2):
                    to = slice((2 * n + b) * CAP, (2 * n + b + 1) * CAP)
                    at = slice((4 * b + q) * CAP, (4 * b + q + 1) * CAP)
                    if n < 7:
                        x[to, :] = x_refs[n][at, :]
                    else:
                        x[to, :half] = x_refs[7][at, :]
                        x[to, half:] = x_refs[8][at, :]
            rows = x[...]
            for m in range(4):
                cut = slice(m * 256, (m + 1) * 256)
                part = dot(rows, w_refs[m // 2][m % 2])
                sums[:, cut] = part if q == 0 else sums[:, cut] + part

        @pl.when(step == 4 + q)
        def _(q=q):
            if q == 0:
                for c in range(2):
                    gate, up = (sums[:, (2 * c + k) * 256 : (2 * c + k + 1) * 256] for k in range(2))
                    inner[:, c * 256 : (c + 1) * 256] = (
                        gate / (1.0 + jnp.exp(-gate)) * up
                    ).astype(BF)
            result = dot(inner[:, :256], down_refs[0][...])
            result = result + dot(inner[:, 256:], down_refs[1][...])
            for n in range(8):
                for b in range(2):
                    at = (2 * n + b) * CAP
                    to = slice((4 * b + q) * CAP, (4 * b + q + 1) * CAP)
                    out_refs[n][to, :] = result[at : at + CAP].astype(BF)


def expert(blocks, own, other, down, other_down):
    rows = 16 * CAP
    block = pl.BlockSpec((BLOCK, QUARTER), lambda j: (0, 0))
    part = pl.BlockSpec((BLOCK, QUARTER // 2), lambda j: (0, 0))
    wide = pl.BlockSpec((2, QUARTER, 256), lambda j: (0, jnp.minimum(j, 3), 0))
    narrow = pl.BlockSpec((256, QUARTER), lambda j: (0, jnp.maximum(j - 4, 0)))
    return pl.pallas_call(
        expert_body,
        grid=(8,),
        out_shape=[shape(BLOCK, QUARTER)] * 8,
        in_specs=[block] * 7 + [part] * 2 + [wide] * 2 + [narrow] * 2,
        out_specs=[block] * 8,
        scratch_shapes=[
            pltpu.VMEM((rows, QUARTER), BF),
            pltpu.VMEM((rows, QUARTER), F32),
            pltpu.VMEM((rows, 512), BF),
        ],
        compiler_params=pltpu.CompilerParams(vmem_limit_bytes=40 << 20),
        cost_estimate=pl.CostEstimate(
            flops=4 << 30, bytes_accessed=14 << 20, transcendentals=0
        ),
        name="expert",
    )(*blocks, own, other, down, other_down)


def gate_body(own_ref, right_ref, left_ref, gate_ref, send_ref):
    target = lax.broadcasted_iota(jnp.int32, (CAP, BLOCK // 2), 0)
    source = lax.broadcasted_iota(jnp.int32, (CAP, BLOCK // 2), 1)
    take = [jnp.where(target + CAP * q == source, 1.0, 0.0).astype(BF) for q in range(4)]
    for x in range(2):
        rows = slice(x * BLOCK // 2, (x + 1) * BLOCK // 2)
        total = own_ref[rows, :].astype(F32) + right_ref[rows, :].astype(F32)
        total = total + left_ref[rows, :].astype(F32)
        total = (total * gate_ref[rows, 0:1]).astype(BF)
        for h in range(8):
            cut = slice(h % 2 * 512, h % 2 * 512 + 512)
            send_ref[x * 8 + h] = dot(take[h // 2], total[:, cut]).astype(BF)


def combine_body(hidden_ref, code_ref, got_ref, out_ref):
    total = hidden_ref[...]
    rows = total.shape[0]
    one, two = code_ref[:, 0:1], code_ref[:, 1:2]
    lane = lax.broadcasted_iota(jnp.int32, (rows, CAP), 1)
    for e in range(E):
        at = lane + e * SLOT
        hot = jnp.where((one == at) | (two == at), 1.0, 0.0).astype(BF)
        total = total + dot(hot, got_ref[e]) + dot(hot, got_ref[8 + e])
    out_ref[0] = total[: rows // 2].astype(BF)
    out_ref[1] = total[rows // 2 :].astype(BF)


def shards(
    queries,
    new_kv,
    cache,
    sinks,
    lengths,
    offsets,
    order,
    residual,
    o_weight,
    ffn_gain,
    router,
    expert_ids,
    w_in,
    w_out,
):
    seq = lax.axis_index(SEQ).astype(jnp.int32).reshape(1)
    core = lax.axis_index("c").astype(jnp.int32).reshape(1)
    swap = [(0, 1), (1, 0)]
    right = [(i, (i + 1) % NZ) for i in range(NZ)]
    left = [(i, (i - 1) % NZ) for i in range(NZ)]
    order_row = order.reshape(1, -1)

    asked = call(
        permute_body,
        shape(32 * ASK, HD),
        "permute",
        3,
        scratch=[pltpu.VMEM((32 * ASK, HD), F32)],
    )(order_row, queries, new_kv)
    w_in, w_out = w_in[0], w_out[0]
    rows = lax.all_to_all(asked, SEQ, split_axis=0, concat_axis=0, tiled=True)

    o_other = lax.ppermute(o_weight, "xh", swap)
    xh = lax.axis_index("xh").astype(jnp.int32).reshape(1)
    o_pair = call(
        pair_body, shape(2, *o_weight.shape), "pair", 3, scalars=1, after=1, nbytes=1 << 19
    )(xh, o_weight, o_other, asked)
    o_all = lax.all_gather(o_pair, "z", axis=0, tiled=False)

    cache_rows = cache.reshape(8192, HD)
    keys, values = split_cycle(cache_rows)
    w_own = unmix(w_in, asked)
    attended, new, w_own = call(
        attend_body,
        [shape(256, HD), shape(128, HD), shape(2, D, 256)],
        "attend",
        7,
        scalars=3,
        after=1,
        keep=True,
        flops=1 << 30,
        nbytes=2 << 20,
        scratch=[
            pltpu.VMEM((256, 4096), F32),
            pltpu.VMEM((8, HD), F32),
            pltpu.VMEM((32 * ASK, HD), F32),
            pltpu.VMEM((256, HD), F32),
        ],
    )(seq, lengths, offsets, rows, sinks.reshape(32, 8, HD), keys, values, w_own)

    owned = lax.all_to_all(attended, SEQ, split_axis=0, concat_axis=0, tiled=True)
    owned_other = lax.ppermute(owned, "c", swap)
    w_other = lax.ppermute(w_own, "c", swap)
    w_out_other = lax.ppermute(w_out, "c", swap)
    share = project(core, owned, owned_other, o_all)
    share = lax.all_to_all(
        share.reshape(16, 64, 256), ("c",) + HEAD, split_axis=0, concat_axis=0, tiled=True
    )
    ids_t = expert_ids.transpose(0, 2, 1)
    hidden, codes, send = call(
        dispatch_body,
        [shape(64, 512, dtype=F32), shape(64, HD, dtype=jnp.int32), shape(16, CAP, 640)],
        "dispatch",
        7,
        flops=1 << 26,
        nbytes=2 << 20,
    )(order_row, share, residual, ffn_gain.reshape(1, -1), router, expert_ids, ids_t)
    cache_out, written = write_cycle(seq, offsets, new, cache_rows, send)
    got = lax.all_to_all(send, ("xh",) + HEAD, split_axis=0, concat_axis=0, tiled=True)
    x, gate = call(
        norm_body,
        [shape(BLOCK, QUARTER), shape(BLOCK, HD, dtype=F32)],
        "norm",
        1,
        after=1,
        flops=1 << 26,
        nbytes=1 << 20,
    )(got, written)

    half = QUARTER // 2
    from_left, from_right = [x], [x]
    for _ in range(3):
        from_left.append(lax.ppermute(from_left[-1], "z", right))
        from_right.append(lax.ppermute(from_right[-1], "z", left))
    far_left = lax.ppermute(from_left[3][:, :half], "z", right)
    far_right = lax.ppermute(from_right[3][:, half:], "z", left)
    blocks = [x] + from_left[1:] + from_right[1:] + [far_left, far_right]
    weights = [
        pltpu.with_memory_space_constraint(w, pltpu.HBM)
        for w in (w_own, w_other, w_out, w_out_other)
    ]
    parts = expert(blocks, *weights)
    own, at_left, at_right, far = parts[0], parts[1:4], parts[4:7], parts[7]

    def add(a, b):
        return (a.astype(F32) + b.astype(F32)).astype(BF)

    to_right = lax.ppermute(far[:, :half], "z", right)
    to_left = lax.ppermute(far[:, half:], "z", left)
    to_right = jnp.concatenate(
        [add(at_right[2][:, :half], to_right), at_right[2][:, half:]], 1
    )
    to_left = jnp.concatenate([at_left[2][:, :half], add(at_left[2][:, half:], to_left)], 1)
    for n in (1, 0):
        to_right = add(at_right[n], lax.ppermute(to_right, "z", right))
        to_left = add(at_left[n], lax.ppermute(to_left, "z", left))
    to_right = lax.ppermute(to_right, "z", right)
    to_left = lax.ppermute(to_left, "z", left)
    back = call(
        gate_body, shape(16, CAP, 512), "gate", 4, flops=1 << 26, nbytes=2 << 20
    )(own, to_right, to_left, gate)
    back = lax.all_to_all(back, ("xh",) + HEAD, split_axis=0, concat_axis=0, tiled=True)
    layer_out = call(
        combine_body, shape(2, 32, 512), "combine", 3, flops=1 << 26, nbytes=1 << 20
    )(hidden, codes, back)
    return (layer_out, cache_out.reshape(cache.shape))


def solution(mesh):
    fine = Mesh(mesh.devices.reshape(2, NZ, 2, 2, 4), SEQ + HEAD)
    return jax.shard_map(
        shards,
        mesh=fine,
        in_specs=(
            P(SEQ, None, HEAD),
            P(SEQ, None, None, HEAD),
            P(SEQ, None, None, HEAD),
            P(None, None, None, HEAD),
            P(),
            P(),
            P(),
            P(SEQ, None, HEAD),
            P(HEAD, SEQ),
            P(HEAD),
            P(HEAD, None),
            P(SEQ, None, None),
            P(HEAD, None, None, SEQ),
            P(HEAD, SEQ, None),
        ),
        out_specs=(P(SEQ, None, HEAD), P(SEQ, None, None, HEAD)),
        check_vma=False,
    )
```

```python
import functools

import jax
import jax.numpy as jnp
from jax import lax
from jax.experimental import pallas as pl
from jax.experimental.pallas import tpu as pltpu
from jax.sharding import Mesh
from jax.sharding import PartitionSpec as P

D = 4096
HD = 128
E = 8
CAP = 18
SLOT = 24
NZ = 8
BF = jnp.bfloat16
F32 = jnp.float32
VMEM = pl.BlockSpec(memory_space=pltpu.VMEM)
ANY = pl.BlockSpec(memory_space=pl.ANY)
HBM = pl.BlockSpec(memory_space=pltpu.HBM)
SMEM = pl.BlockSpec(memory_space=pltpu.SMEM)
SEQ = ("xh", "z", "c")
HEAD = ("xl", "y")


def call(
    body, outs, name, n_in, scalars=0, after=0, flops=0, nbytes=0, limit=20, scratch=(), keep=False
):
    return pl.pallas_call(
        body,
        out_shape=outs,
        in_specs=[SMEM] * scalars
        + [VMEM] * (n_in - scalars)
        + [HBM if keep else ANY] * after,
        out_specs=[VMEM] * (len(outs) - 1) + [HBM]
        if keep
        else jax.tree.map(lambda _: VMEM, outs),
        input_output_aliases={n_in + after - 1: len(outs) - 1} if keep else {},
        scratch_shapes=list(scratch),
        compiler_params=pltpu.CompilerParams(vmem_limit_bytes=limit << 20),
        cost_estimate=pl.CostEstimate(
            flops=flops, bytes_accessed=nbytes, transcendentals=0
        ),
        name=name,
    )


def shape(*dims, dtype=BF):
    return jax.ShapeDtypeStruct(dims, dtype)


def dot(a, b):
    return jnp.dot(a, b, preferred_element_type=F32)


def dot_t(a, b):
    return lax.dot_general(a, b, (((1,), (1,)), ((), ())), preferred_element_type=F32)


def slot_of_request(order_row):
    n = order_row.shape[1]
    return order_row == lax.broadcasted_iota(jnp.int32, (n, n), 0)


ASK = 16


def permute_body(order_ref, q_ref, kv_ref, out_ref, wide):
    hot = jnp.where(slot_of_request(order_ref[...]), 1.0, 0.0).astype(BF)
    count = hot.shape[0]
    wide[...] = jnp.zeros_like(wide)
    for i in range(2):
        rows = jnp.concatenate([q_ref[i], kv_ref[i, :, 0, :], kv_ref[i, :, 1, :]], 1)
        rows = dot(hot, rows)
        for g in range(6):
            wide[pl.ds(i * 6 + g, count, stride=ASK), :] = rows[:, g * HD : (g + 1) * HD]
    out_ref[...] = wide[...].astype(BF)


def split_body(cache_ref, k_ref, v_ref, wide):
    rows = cache_ref.shape[0]
    wide[...] = cache_ref[...].astype(F32)
    k_ref[...] = wide[pl.ds(0, rows // 2, stride=2), :].astype(BF)
    v_ref[...] = wide[pl.ds(1, rows // 2, stride=2), :].astype(BF)


def split_cycle(cache_rows):
    rows = cache_rows.shape[0]
    return call(
        split_body,
        [shape(rows // 2, HD)] * 2,
        "split_cycle",
        1,
        flops=1 << 24,
        nbytes=8 << 20,
        scratch=[pltpu.VMEM((rows, HD), F32)],
    )(cache_rows)


CHUNK = 512


def attend_body(
    seq_ref,
    len_ref,
    off_ref,
    rows_ref,
    sink_ref,
    k_ref,
    v_ref,
    weight_ref,
    out_ref,
    new_ref,
    weight_out_ref,
    scores,
    wide,
    asked,
    mixed_rows,
):
    seq = seq_ref[0]
    length, offset = len_ref[seq], off_ref[seq]
    half = rows_ref.shape[0] // ASK
    span = 2 * half
    cycle = k_ref.shape[0]
    group = 4
    asked[...] = rows_ref[...].astype(F32)

    def piece(g):
        return jnp.concatenate(
            [asked[pl.ds(i * 6 + g, half, stride=ASK), :] for i in range(2)], 0
        )

    query = jnp.concatenate([piece(g) for g in range(group)], 0).astype(BF)
    new_k, new_v = piece(4), piece(5)
    new_ref[...] = jnp.concatenate([new_k, new_v], 0).astype(BF)
    count = span * group
    scale = HD**-0.5
    row = lax.broadcasted_iota(jnp.int32, (count, 1), 0) % span
    token = row % half * 2 + row // half
    oldest = jnp.maximum(token + 1, cycle - length + 4)
    wide[...] = sink_ref[seq].astype(F32)
    pad = jnp.zeros((span - 4, HD), F32)
    first_k = jnp.concatenate([wide[pl.ds(0, 4, stride=2), :], pad, new_k], 0).astype(BF)
    first_v = jnp.concatenate([wide[pl.ds(1, 4, stride=2), :], pad, new_v], 0).astype(BF)
    column = lax.broadcasted_iota(jnp.int32, (1, 2 * span), 1)
    at = column - span
    live = (column < 4) | ((at >= 0) & (at % half * 2 + at // half <= token))
    low = jnp.float32(-jnp.inf)
    first = jnp.where(live, dot_t(query, first_k), low)
    peak = first
    for n in range(cycle // CHUNK):
        part = dot_t(query, k_ref[n * CHUNK : (n + 1) * CHUNK, :])
        age = lax.broadcasted_iota(jnp.int32, (1, CHUNK), 1) + (n * CHUNK - offset)
        age = jnp.where(age < 0, age + cycle, age)
        part = jnp.where(age >= oldest, part, low)
        scores[:, n * CHUNK : (n + 1) * CHUNK] = part
        for m in range(CHUNK // HD):
            peak = jnp.maximum(peak, part[:, m * HD : (m + 1) * HD])
    top = jnp.max(peak, 1, keepdims=True)
    expo = jnp.exp((first - top) * scale)
    total = expo
    acc = dot(expo.astype(BF), first_v)
    for n in range(cycle // CHUNK):
        expo = jnp.exp((scores[:, n * CHUNK : (n + 1) * CHUNK] - top) * scale)
        for m in range(CHUNK // HD):
            total = total + expo[:, m * HD : (m + 1) * HD]
        acc = acc + dot(expo.astype(BF), v_ref[n * CHUNK : (n + 1) * CHUNK, :])
    mixed = acc / jnp.sum(total, 1, keepdims=True)
    for g in range(group):
        for i in range(2):
            first_row = g * span + i * half
            mixed_rows[pl.ds(i * 4 + g, half, stride=8), :] = mixed[
                first_row : first_row + half
            ]
    out_ref[...] = mixed_rows[...].astype(BF)


WINDOW = 144


def write_body(seq_ref, off_ref, new_ref, cache_ref, after_ref, out_ref, done_ref):
    done_ref[...] = jnp.zeros_like(done_ref)
    offset = off_ref[seq_ref[0]]
    step = cache_ref.shape[0]
    total = step * pl.num_programs(0)
    span = new_ref.shape[0] // 2
    half = span // 2
    out_ref[...] = cache_ref[...]
    for wrap in (0, 1):
        first = 2 * offset - wrap * total - pl.program_id(0) * step

        @pl.when((first > -2 * span) & (first < step))
        def _(first=first):
            start = jnp.clip(first, 0, step - WINDOW) // 16 * 16
            window = pl.ds(pl.multiple_of(start, 16), WINDOW)
            row = lax.broadcasted_iota(jnp.int32, (WINDOW, 1), 0) + start
            at = row - first
            column = lax.broadcasted_iota(jnp.int32, (1, 2 * span), 1)
            hot = at % 2 * span + at // 2 % 2 * half + at // 4 == column
            written = (at >= 0) & (at < 2 * span)
            hot = jnp.where(written & hot, 1.0, 0.0).astype(BF)
            fresh = dot(hot, new_ref[...])
            old = out_ref[window, :].astype(F32)
            out_ref[window, :] = jnp.where(written, fresh, old).astype(BF)


def write_cycle(seq, offsets, new, cache_rows, after):
    total, step = cache_rows.shape[0], 2048
    return pl.pallas_call(
        write_body,
        grid=(total // step,),
        out_shape=[shape(total, HD), shape(8, HD, dtype=F32)],
        in_specs=[
            SMEM,
            SMEM,
            pl.BlockSpec(new.shape, lambda n: (0, 0)),
            pl.BlockSpec((step, HD), lambda n: (n, 0)),
            ANY,
        ],
        out_specs=[
            pl.BlockSpec((step, HD), lambda n: (n, 0)),
            pl.BlockSpec((8, HD), lambda n: (0, 0)),
        ],
        cost_estimate=pl.CostEstimate(
            flops=1 << 24, bytes_accessed=16 << 20, transcendentals=0
        ),
        compiler_params=pltpu.CompilerParams(vmem_limit_bytes=16 << 20),
        name="write_cycle",
    )(seq, offsets, new, cache_rows, after)


def pair_body(xh_ref, own_ref, other_ref, after_ref, out_ref):
    xh = xh_ref[0]
    out_ref[xh] = own_ref[...]
    out_ref[1 - xh] = other_ref[...]


def pass_body(first_ref, weight_ref, out_ref, weight_out_ref):
    out_ref[...] = first_ref[0:8, :]


def unmix_body(w_ref, after_ref, out_ref):
    for k in range(2):
        out_ref[k] = w_ref[:, k, :]


def unmix(w_in, after):
    step = 512
    return pl.pallas_call(
        unmix_body,
        grid=(D // step,),
        out_shape=shape(2, D, 256),
        in_specs=[pl.BlockSpec((step, 2, 256), lambda n: (n, 0, 0)), ANY],
        out_specs=pl.BlockSpec((2, step, 256), lambda n: (0, n, 0)),
        cost_estimate=pl.CostEstimate(
            flops=1 << 20, bytes_accessed=16 << 20, transcendentals=0
        ),
        compiler_params=pltpu.CompilerParams(vmem_limit_bytes=16 << 20),
        name="unmix",
    )(w_in, after)


def project_body(core_ref, own_ref, other_ref, w_ref, out_ref, wide, both):
    half = own_ref.shape[0] // 8
    rows = 2 * half

    @pl.when(pl.program_id(0) == 0)
    def _():
        first = core_ref[0] == 0
        own, other = own_ref[...].astype(F32), other_ref[...].astype(F32)
        for c in range(2):
            wide[...] = jnp.where(first == (c == 0), own, other)
            for i in range(2):
                for g in range(4):
                    at = c * rows + i * half
                    both[at : at + half, g * HD : (g + 1) * HD] = wide[
                        pl.ds(i * 4 + g, half, stride=8), :
                    ].astype(BF)

    for n in range(2):
        weight = jnp.concatenate([w_ref[2 * n, 0], w_ref[2 * n + 1, 0]], 1)
        result = dot(both[...], weight).astype(BF)
        out_ref[0, n] = result[:rows]
        out_ref[1, n] = result[rows:]


def project(core, own, other, weight):
    rows = own.shape[0] // 4
    return pl.pallas_call(
        project_body,
        grid=(4,),
        out_shape=shape(2, 8, rows, 256),
        in_specs=[
            SMEM,
            pl.BlockSpec(own.shape, lambda n: (0, 0)),
            pl.BlockSpec(own.shape, lambda n: (0, 0)),
            pl.BlockSpec((4, 1, 512, 128), lambda n: (n % 2, n // 2, 0, 0)),
        ],
        out_specs=pl.BlockSpec((2, 2, rows, 256), lambda n: (0, n, 0, 0)),
        scratch_shapes=[pltpu.VMEM(own.shape, F32), pltpu.VMEM((2 * rows, 512), BF)],
        cost_estimate=pl.CostEstimate(
            flops=1 << 28, bytes_accessed=3 << 20, transcendentals=0
        ),
        compiler_params=pltpu.CompilerParams(vmem_limit_bytes=16 << 20),
        name="project",
    )(core, own, other, weight)


def pieces(value):
    high = value.astype(BF).astype(F32)
    rest = value - high
    middle = rest.astype(BF).astype(F32)
    return high, middle, (rest - middle).astype(BF).astype(F32)


def dispatch_body(
    order_ref,
    part_ref,
    res_ref,
    gain_ref,
    router_ref,
    ids_ref,
    ids_t_ref,
    hidden_ref,
    code_ref,
    send_ref,
):
    hot = jnp.where(slot_of_request(order_ref[...]), 1.0, 0.0).astype(BF)
    resid = jnp.concatenate([dot(hot, res_ref[i]) for i in range(2)], 0)
    picks = jnp.concatenate(
        [dot(hot, ids_ref[i].astype(F32).astype(BF)) for i in range(2)], 0
    )
    picks_t = jnp.concatenate(
        [dot_t(ids_t_ref[i].astype(F32).astype(BF), hot) for i in range(2)], 1
    )
    sums = []
    for c in range(2):
        total = part_ref[c * 8].astype(F32)
        for h in range(1, 8):
            total = total + part_ref[c * 8 + h].astype(F32)
        sums.append(total)
    projected = jnp.concatenate(
        [sums[0][:, :HD], sums[1][:, :HD], sums[0][:, HD:], sums[1][:, HD:]], 1
    )
    hidden = resid + projected
    hidden_ref[...] = hidden
    gained = hidden * gain_ref[...]
    square = jnp.sum(hidden * hidden, 1, keepdims=True)
    share = jnp.dot(
        gained,
        router_ref[...],
        precision=lax.Precision.HIGHEST,
        preferred_element_type=F32,
    )
    rows = hidden.shape[0]
    one, two = picks[:, 0:1], picks[:, 1:2]
    expert = lax.broadcasted_iota(jnp.int32, (1, E), 1).astype(F32)
    first, second = one == expert, two == expert
    apart = jnp.sum(jnp.where(first, share, 0.0) - jnp.where(second, share, 0.0), 1, keepdims=True)
    before = lax.broadcasted_iota(jnp.int32, (rows, rows), 0)
    after = lax.broadcasted_iota(jnp.int32, (rows, rows), 1)
    lower = jnp.where(before > after, 1.0, 0.0).astype(BF)
    upper = jnp.where(before < after, 1.0, 0.0).astype(BF)
    earlier = dot(lower, jnp.where(first | second, 1.0, 0.0).astype(BF))
    slot_one = jnp.sum(jnp.where(first, earlier, 0.0), 1, keepdims=True)
    slot_two = jnp.sum(jnp.where(second, earlier, 0.0), 1, keepdims=True)
    lane = lax.broadcasted_iota(jnp.int32, (rows, HD), 1)
    code_ref[...] = jnp.where(
        lane == 0, one * SLOT + slot_one, two * SLOT + slot_two
    ).astype(jnp.int32)
    one_t, two_t = picks_t[0:1], picks_t[1:2]
    expert_t = lax.broadcasted_iota(jnp.int32, (E, 1), 0).astype(F32)
    first_t, second_t = one_t == expert_t, two_t == expert_t
    earlier_t = dot(jnp.where(first_t | second_t, 1.0, 0.0).astype(BF), upper)
    slot_one_t = jnp.sum(jnp.where(first_t, earlier_t, 0.0), 0, keepdims=True)
    slot_two_t = jnp.sum(jnp.where(second_t, earlier_t, 0.0), 0, keepdims=True)
    place = lax.broadcasted_iota(jnp.int32, (E * SLOT, 1), 0).astype(F32)
    is_one = jnp.where(place == one_t * SLOT + slot_one_t, 1.0, 0.0)
    is_two = jnp.where(place == two_t * SLOT + slot_two_t, 1.0, 0.0)
    plus, minus = (is_one + is_two).astype(BF), (is_one - is_two).astype(BF)
    bucket = dot(plus, gained.astype(BF)).astype(BF)
    norm_terms, gate_terms = jnp.zeros((rows, HD), F32), jnp.zeros((rows, HD), F32)
    for n, (s, a) in enumerate(zip(pieces(square), pieces(apart))):
        norm_terms = jnp.where(lane == n, s, norm_terms)
        gate_terms = jnp.where(lane == 3 + n, a, gate_terms)
    terms = (dot(plus, norm_terms.astype(BF)) + dot(minus, gate_terms.astype(BF))).astype(BF)
    for e in range(E):
        for x in range(2):
            send_ref[x * E + e, :, 0:512] = bucket[e * SLOT : e * SLOT + CAP]
            send_ref[x * E + e, :, 512:640] = terms[e * SLOT : e * SLOT + CAP]


QUARTER = D // 4
BLOCK = 8 * CAP


def norm_body(got_ref, after_ref, x_ref, gate_ref):
    target = lax.broadcasted_iota(jnp.int32, (BLOCK, CAP), 0)
    source = lax.broadcasted_iota(jnp.int32, (BLOCK, CAP), 1)
    lane = lax.broadcasted_iota(jnp.int32, (CAP, HD), 1)
    parts, gates = [0.0, 0.0], 0.0
    for x in range(2):
        terms = got_ref[x * 8, :, 512:640].astype(F32)
        for h in range(1, 8):
            terms = terms + got_ref[x * 8 + h, :, 512:640].astype(F32)
        square = jnp.sum(jnp.where(lane < 3, terms, 0.0), 1, keepdims=True)
        apart = jnp.sum(jnp.where((lane >= 3) & (lane < 6), terms, 0.0), 1, keepdims=True)
        inv_rms = lax.rsqrt(square / D + 1e-05)
        gate = 1.0 / (1.0 + jnp.exp(-(apart * inv_rms)))
        gate = jnp.broadcast_to(gate, (CAP, HD)).astype(BF)
        for q in range(4):
            put = jnp.where(target == source + CAP * (4 * x + q), 1.0, 0.0).astype(BF)
            gates = gates + dot(put, gate)
            for n in range(2):
                rows = got_ref[x * 8 + 2 * q + n, :, 0:512].astype(F32) * inv_rms
                parts[n] = parts[n] + dot(put, rows.astype(BF))
    gate_ref[...] = gates
    for n in range(2):
        x_ref[:, n * 512 : (n + 1) * 512] = parts[n].astype(BF)


def expert_body(*refs):
    x_refs, refs = refs[:9], refs[9:]
    w_refs, down_refs = refs[0:2], refs[2:4]
    out_refs, (x, sums, inner) = refs[4:12], refs[12:]
    half = QUARTER // 2
    step = pl.program_id(0)
    for q in range(4):

        @pl.when(step == q)
        def _(q=q):
            for n in range(8):
                for b in range(2):
                    to = slice((2 * n + b) * CAP, (2 * n + b + 1) * CAP)
                    at = slice((4 * b + q) * CAP, (4 * b + q + 1) * CAP)
                    if n < 7:
                        x[to, :] = x_refs[n][at, :]
                    else:
                        x[to, :half] = x_refs[7][at, :]
                        x[to, half:] = x_refs[8][at, :]
            rows = x[...]
            for m in range(4):
                cut = slice(m * 256, (m + 1) * 256)
                part = dot(rows, w_refs[m // 2][m % 2])
                sums[:, cut] = part if q == 0 else sums[:, cut] + part

        @pl.when(step == 4 + q)
        def _(q=q):
            if q == 0:
                for c in range(2):
                    gate, up = (sums[:, (2 * c + k) * 256 : (2 * c + k + 1) * 256] for k in range(2))
                    inner[:, c * 256 : (c + 1) * 256] = (
                        gate / (1.0 + jnp.exp(-gate)) * up
                    ).astype(BF)
            result = dot(inner[:, :256], down_refs[0][...])
            result = result + dot(inner[:, 256:], down_refs[1][...])
            for n in range(8):
                for b in range(2):
                    at = (2 * n + b) * CAP
                    to = slice((4 * b + q) * CAP, (4 * b + q + 1) * CAP)
                    out_refs[n][to, :] = result[at : at + CAP].astype(BF)


def expert(blocks, own, other, down, other_down):
    rows = 16 * CAP
    block = pl.BlockSpec((BLOCK, QUARTER), lambda j: (0, 0))
    part = pl.BlockSpec((BLOCK, QUARTER // 2), lambda j: (0, 0))
    wide = pl.BlockSpec((2, QUARTER, 256), lambda j: (0, jnp.minimum(j, 3), 0))
    narrow = pl.BlockSpec((256, QUARTER), lambda j: (0, jnp.maximum(j - 4, 0)))
    return pl.pallas_call(
        expert_body,
        grid=(8,),
        out_shape=[shape(BLOCK, QUARTER)] * 8,
        in_specs=[block] * 7 + [part] * 2 + [wide] * 2 + [narrow] * 2,
        out_specs=[block] * 8,
        scratch_shapes=[
            pltpu.VMEM((rows, QUARTER), BF),
            pltpu.VMEM((rows, QUARTER), F32),
            pltpu.VMEM((rows, 512), BF),
        ],
        compiler_params=pltpu.CompilerParams(vmem_limit_bytes=40 << 20),
        cost_estimate=pl.CostEstimate(
            flops=4 << 30, bytes_accessed=14 << 20, transcendentals=0
        ),
        name="expert",
    )(*blocks, own, other, down, other_down)


def gate_body(own_ref, right_ref, left_ref, gate_ref, send_ref):
    target = lax.broadcasted_iota(jnp.int32, (CAP, BLOCK // 2), 0)
    source = lax.broadcasted_iota(jnp.int32, (CAP, BLOCK // 2), 1)
    take = [jnp.where(target + CAP * q == source, 1.0, 0.0).astype(BF) for q in range(4)]
    for x in range(2):
        rows = slice(x * BLOCK // 2, (x + 1) * BLOCK // 2)
        total = own_ref[rows, :].astype(F32) + right_ref[rows, :].astype(F32)
        total = total + left_ref[rows, :].astype(F32)
        total = (total * gate_ref[rows, 0:1]).astype(BF)
        for h in range(8):
            cut = slice(h % 2 * 512, h % 2 * 512 + 512)
            send_ref[x * 8 + h] = dot(take[h // 2], total[:, cut]).astype(BF)


def combine_body(hidden_ref, code_ref, got_ref, out_ref):
    total = hidden_ref[...]
    rows = total.shape[0]
    one, two = code_ref[:, 0:1], code_ref[:, 1:2]
    lane = lax.broadcasted_iota(jnp.int32, (rows, CAP), 1)
    for e in range(E):
        at = lane + e * SLOT
        hot = jnp.where((one == at) | (two == at), 1.0, 0.0).astype(BF)
        total = total + dot(hot, got_ref[e]) + dot(hot, got_ref[8 + e])
    out_ref[0] = total[: rows // 2].astype(BF)
    out_ref[1] = total[rows // 2 :].astype(BF)


def shards(
    queries,
    new_kv,
    cache,
    sinks,
    lengths,
    offsets,
    order,
    residual,
    o_weight,
    ffn_gain,
    router,
    expert_ids,
    w_in,
    w_out,
):
    seq = lax.axis_index(SEQ).astype(jnp.int32).reshape(1)
    core = lax.axis_index("c").astype(jnp.int32).reshape(1)
    swap = [(0, 1), (1, 0)]
    right = [(i, (i + 1) % NZ) for i in range(NZ)]
    left = [(i, (i - 1) % NZ) for i in range(NZ)]
    order_row = order.reshape(1, -1)

    asked = call(
        permute_body,
        shape(32 * ASK, HD),
        "permute",
        3,
        scratch=[pltpu.VMEM((32 * ASK, HD), F32)],
    )(order_row, queries, new_kv)
    w_in, w_out = w_in[0], w_out[0]
    rows = lax.all_to_all(asked, SEQ, split_axis=0, concat_axis=0, tiled=True)

    o_other = lax.ppermute(o_weight, "xh", swap)
    xh = lax.axis_index("xh").astype(jnp.int32).reshape(1)
    o_pair = call(
        pair_body, shape(2, *o_weight.shape), "pair", 3, scalars=1, after=1, nbytes=1 << 19
    )(xh, o_weight, o_other, asked)
    o_all = lax.all_gather(o_pair, "z", axis=0, tiled=False)

    cache_rows = cache.reshape(8192, HD)
    keys, values = split_cycle(cache_rows)
    w_own = unmix(w_in, asked)
    attended, new, w_own = call(
        attend_body,
        [shape(256, HD), shape(128, HD), shape(2, D, 256)],
        "attend",
        7,
        scalars=3,
        after=1,
        keep=True,
        flops=1 << 30,
        nbytes=2 << 20,
        scratch=[
            pltpu.VMEM((256, 4096), F32),
            pltpu.VMEM((8, HD), F32),
            pltpu.VMEM((32 * ASK, HD), F32),
            pltpu.VMEM((256, HD), F32),
        ],
    )(seq, lengths, offsets, rows, sinks.reshape(32, 8, HD), keys, values, w_own)

    owned = lax.all_to_all(attended, SEQ, split_axis=0, concat_axis=0, tiled=True)
    owned_other = lax.ppermute(owned, "c", swap)
    w_out_other = lax.ppermute(w_out, "c", swap)
    _, w_own = call(
        pass_body, [shape(8, HD), shape(2, D, 256)], "pass_on", 1, after=1, keep=True
    )(owned_other.reshape(-1, HD), w_own)
    w_other = lax.ppermute(w_own, "c", swap)
    share = project(core, owned, owned_other, o_all)
    share = lax.all_to_all(
        share.reshape(16, 64, 256), ("c",) + HEAD, split_axis=0, concat_axis=0, tiled=True
    )
    ids_t = expert_ids.transpose(0, 2, 1)
    hidden, codes, send = call(
        dispatch_body,
        [shape(64, 512, dtype=F32), shape(64, HD, dtype=jnp.int32), shape(16, CAP, 640)],
        "dispatch",
        7,
        flops=1 << 26,
        nbytes=2 << 20,
    )(order_row, share, residual, ffn_gain.reshape(1, -1), router, expert_ids, ids_t)
    cache_out, written = write_cycle(seq, offsets, new, cache_rows, send)
    got = lax.all_to_all(send, ("xh",) + HEAD, split_axis=0, concat_axis=0, tiled=True)
    x, gate = call(
        norm_body,
        [shape(BLOCK, QUARTER), shape(BLOCK, HD, dtype=F32)],
        "norm",
        1,
        after=1,
        flops=1 << 26,
        nbytes=1 << 20,
    )(got, written)

    half = QUARTER // 2
    from_left, from_right = [x], [x]
    for _ in range(3):
        from_left.append(lax.ppermute(from_left[-1], "z", right))
        from_right.append(lax.ppermute(from_right[-1], "z", left))
    far_left = lax.ppermute(from_left[3][:, :half], "z", right)
    far_right = lax.ppermute(from_right[3][:, half:], "z", left)
    blocks = [x] + from_left[1:] + from_right[1:] + [far_left, far_right]
    weights = [
        pltpu.with_memory_space_constraint(w, pltpu.HBM)
        for w in (w_own, w_other, w_out, w_out_other)
    ]
    parts = expert(blocks, *weights)
    own, at_left, at_right, far = parts[0], parts[1:4], parts[4:7], parts[7]

    def add(a, b):
        return (a.astype(F32) + b.astype(F32)).astype(BF)

    to_right = lax.ppermute(far[:, :half], "z", right)
    to_left = lax.ppermute(far[:, half:], "z", left)
    to_right = jnp.concatenate(
        [add(at_right[2][:, :half], to_right), at_right[2][:, half:]], 1
    )
    to_left = jnp.concatenate([at_left[2][:, :half], add(at_left[2][:, half:], to_left)], 1)
    for n in (1, 0):
        to_right = add(at_right[n], lax.ppermute(to_right, "z", right))
        to_left = add(at_left[n], lax.ppermute(to_left, "z", left))
    to_right = lax.ppermute(to_right, "z", right)
    to_left = lax.ppermute(to_left, "z", left)
    back = call(
        gate_body, shape(16, CAP, 512), "gate", 4, flops=1 << 26, nbytes=2 << 20
    )(own, to_right, to_left, gate)
    back = lax.all_to_all(back, ("xh",) + HEAD, split_axis=0, concat_axis=0, tiled=True)
    layer_out = call(
        combine_body, shape(2, 32, 512), "combine", 3, flops=1 << 26, nbytes=1 << 20
    )(hidden, codes, back)
    return (layer_out, cache_out.reshape(cache.shape))


def solution(mesh):
    fine = Mesh(mesh.devices.reshape(2, NZ, 2, 2, 4), SEQ + HEAD)
    return jax.shard_map(
        shards,
        mesh=fine,
        in_specs=(
            P(SEQ, None, HEAD),
            P(SEQ, None, None, HEAD),
            P(SEQ, None, None, HEAD),
            P(None, None, None, HEAD),
            P(),
            P(),
            P(),
            P(SEQ, None, HEAD),
            P(HEAD, SEQ),
            P(HEAD),
            P(HEAD, None),
            P(SEQ, None, None),
            P(HEAD, None, None, SEQ),
            P(HEAD, SEQ, None),
        ),
        out_specs=(P(SEQ, None, HEAD), P(SEQ, None, None, HEAD)),
        check_vma=False,
    )
```
